32 devices in a mesh: grp: 2 (over y), ctx: 4 (over z), tp: 4 (over x, core).
Axes of the slice: x: 2, y: 2, z: 4, core: 2. Of those that a mesh axis runs over, the one named last changes fastest.
Arguments:
- query_projected: bfloat16 [1536, 2048], P(('grp', 'ctx'), 'tp'), parts along dimension 0, may hold values from -6 to 6
- key_projected: bfloat16 [1536, 2048], P(('grp', 'ctx'), 'tp'), parts along dimension 0, may hold values from -6 to 6
- value_projected: bfloat16 [1536, 2048], P(('grp', 'ctx'), 'tp'), parts along dimension 0, may hold values from -6 to 6
- long_conv_output: bfloat16 [1536, 2048], P(('grp', 'ctx'), 'tp'), parts along dimension 0, may hold values from -6 to 6
- short_conv_filter: float32 [3, 3, 2048], P(None, None, 'tp'), may hold values from -3.5 to 3.5
- direct_bias: float32 [2048], P('tp'), may hold values from -3 to 3
- mode_residue: float32 [2048, 16], P('tp'), may hold values from -1.5 to 1.5
- mode_decay_rate: float32 [2048, 16], P('tp'), may hold values from 0.5 to 25
- output_weight: bfloat16 [2048, 2048], P(None, 'tp'), may hold values from -0.125 to 0.125
- adapter_down_factor: bfloat16 [2048, 16], replicated, may hold values from -0.125 to 0.125
- adapter_up_factor: bfloat16 [16, 2048], P(None, 'tp'), may hold values from -0.125 to 0.125
- output_gradient: bfloat16 [1536, 2048], P(('grp', 'ctx'), 'tp'), parts along dimension 0, may hold values from -6 to 6
Outputs:
- query_input_gradient: bfloat16 [1536, 2048], P(('grp', 'ctx'), 'tp'), parts along dimension 0
- key_input_gradient: bfloat16 [1536, 2048], P(('grp', 'ctx'), 'tp'), parts along dimension 0
- value_input_gradient: bfloat16 [1536, 2048], P(('grp', 'ctx'), 'tp'), parts along dimension 0
- down_factor_gradient: float32 [4096, 16], P(('grp', 'tp')), parts along dimension 0
- up_factor_gradient: float32 [32, 2048], P('grp', 'tp'), parts along dimension 0
The draws below stay inside these ranges and needn't reach their ends.
There are 2 independent parts, one for each index of `grp`. The reference program is written for one: setup_inputs(seed, part) draws one part's arguments, and reference() takes and returns one part's arrays. A program takes and returns all parts, laid end to end along the dimension named above; an argument that names none is the same for every part. Nothing has to cross between parts.
All inputs are finite; a program needn't handle non-finite values.
Results may differ from the reference program's by a relative error of at most 0.013.
Values may be sent and summed in bfloat16 or wider, within the bound.
A program may use at most 64 MiB of HBM per device.

```python
import math
import jax
import jax.numpy as jnp
from jax import lax

MIXER_CHANNELS = 2048
OUTPUT_FEATURES = 2048
ADAPTER_RANK = 16
MODES = 16
SHORT = 3
SEQUENCE_TOKENS = 768
N_TP = 4


def block_scale(stream_key, shape, split, least, top_value):
    loudness = 1.0
    for axis_at, blocks in split:
        steps = jax.random.uniform(jax.random.fold_in(jax.random.fold_in(stream_key, 6), axis_at), (blocks,), jnp.float32, least / len(split), top_value / len(split))
        loudness = loudness * jnp.repeat(jnp.exp(steps), shape[axis_at] // blocks).reshape((-1,) + (1,) * (len(shape) - 1 - axis_at))
    return loudness


def normal_values(stream_key, dims, deviation, limit, cuts=(), held_as=jnp.bfloat16):
    gain = block_scale(stream_key, dims, cuts, -0.22, 0.18) if cuts else 1.0
    array = jax.random.normal(stream_key, dims, jnp.float32) * deviation * gain
    return jnp.minimum(jnp.maximum(array, -limit), limit).astype(held_as)


def setup_inputs(seed: int = 0, part: int = 0) -> dict:
    streams_of = jax.random.split(jax.random.key(seed), 13)
    own_keys = jax.random.split(jax.random.fold_in(streams_of[12], part), 13)
    return {
        "query_projected": normal_values(own_keys[0], (SEQUENCE_TOKENS, MIXER_CHANNELS), 1.0, 6.0, ((0, 4), (1, 4))),
        "key_projected": normal_values(own_keys[1], (SEQUENCE_TOKENS, MIXER_CHANNELS), 1.0, 6.0, ((0, 4), (1, 4))),
        "value_projected": normal_values(own_keys[2], (SEQUENCE_TOKENS, MIXER_CHANNELS), 1.0, 6.0, ((0, 4), (1, 4))),
        "long_conv_output": normal_values(own_keys[3], (SEQUENCE_TOKENS, MIXER_CHANNELS), 1.0, 6.0, ((0, 4), (1, 4))),
        "short_conv_filter": normal_values(streams_of[4], (3, SHORT, MIXER_CHANNELS), SHORT ** -0.5, 3.5, ((2, 4),), jnp.float32),
        "direct_bias": normal_values(streams_of[5], (MIXER_CHANNELS,), 0.5, 3.0, ((0, 4),), jnp.float32),
        "mode_residue": normal_values(streams_of[6], (MIXER_CHANNELS, MODES), 0.25, 1.5, ((0, 4),), jnp.float32),
        "mode_decay_rate": jnp.clip(jnp.exp(math.log(25.0) - 3.912023 * jax.random.uniform(streams_of[7], (MIXER_CHANNELS, MODES), jnp.float32) ** block_scale(streams_of[7], (MIXER_CHANNELS, MODES), ((0, 4),), -0.2, 0.2)), 0.5, 25.0),
        "output_weight": normal_values(streams_of[8], (MIXER_CHANNELS, OUTPUT_FEATURES), MIXER_CHANNELS ** -0.5, 0.125, ((1, 4),)),
        "adapter_down_factor": normal_values(streams_of[9], (MIXER_CHANNELS, ADAPTER_RANK), MIXER_CHANNELS ** -0.5, 0.125),
        "adapter_up_factor": normal_values(streams_of[10], (ADAPTER_RANK, OUTPUT_FEATURES), OUTPUT_FEATURES ** -0.5, 0.125, ((1, 4),)),
        "output_gradient": normal_values(own_keys[11], (SEQUENCE_TOKENS, OUTPUT_FEATURES), 1.0, 6.0, ((0, 4), (1, 4))),
    }


adapter_scale = 2.0
channel_block = 64

def short_forward(signal_pre, taps):
    signal = signal_pre.astype(jnp.float32)
    length = signal.shape[0]
    joined = jnp.concatenate([jnp.zeros((2, signal.shape[1]), jnp.float32), signal], axis=0)
    return taps[0] * joined[2:] + taps[1] * joined[1:length + 1] + taps[2] * joined[0:length]

def short_backward(grad_signal, taps):
    length = grad_signal.shape[0]
    joined = jnp.concatenate([grad_signal, jnp.zeros((2, grad_signal.shape[1]), jnp.float32)], axis=0)
    return taps[0] * joined[0:length] + taps[1] * joined[1:length + 1] + taps[2] * joined[2:]

def long_filter(residue, rate):
    times = jnp.arange(SEQUENCE_TOKENS).astype(jnp.float32)
    weights = residue * jnp.sqrt(rate / SEQUENCE_TOKENS)
    total = jnp.zeros((residue.shape[0], SEQUENCE_TOKENS), jnp.float32)
    for index_mode in range(residue.shape[1]):
        decay = jnp.exp(-(rate[:, index_mode:index_mode + 1] * times[None, :]) / SEQUENCE_TOKENS)
        total = total + weights[:, index_mode:index_mode + 1] * decay
    return total

def correlate(block):
    grad_block, residue, rate = block
    filt = long_filter(residue, rate)
    spec_filter = jnp.fft.fft(filt, n=2 * SEQUENCE_TOKENS, axis=1)
    spec_grad = jnp.fft.fft(grad_block, n=2 * SEQUENCE_TOKENS, axis=1)
    return jnp.real(jnp.fft.ifft(spec_grad * jnp.conj(spec_filter), axis=1))[:, :SEQUENCE_TOKENS]

def reference(query_projected, key_projected, value_projected, long_conv_output, short_conv_filter, direct_bias, mode_residue, mode_decay_rate, output_weight, adapter_down_factor, adapter_up_factor, output_gradient):
    query = short_forward(query_projected, short_conv_filter[0])
    key = short_forward(key_projected, short_conv_filter[1])
    value = short_forward(value_projected, short_conv_filter[2])
    conv_value = long_conv_output.astype(jnp.float32)
    gated_signal = (query * conv_value).astype(jnp.bfloat16)
    adapter_gradient = jnp.dot(output_gradient, adapter_up_factor.T, preferred_element_type=jnp.float32).astype(jnp.bfloat16)
    adapter_activation = jnp.dot(gated_signal, adapter_down_factor, preferred_element_type=jnp.float32).astype(jnp.bfloat16)
    block_width = OUTPUT_FEATURES // N_TP
    gate_gradient = jnp.zeros((SEQUENCE_TOKENS, MIXER_CHANNELS), jnp.float32)
    for index_block in range(N_TP):
        lower = index_block * block_width
        piece = jnp.dot(output_gradient[:, lower:lower + block_width], output_weight[:, lower:lower + block_width].T, preferred_element_type=jnp.float32).astype(jnp.bfloat16)
        gate_gradient = gate_gradient + piece.astype(jnp.float32)
    gate_gradient = gate_gradient + adapter_scale * jnp.dot(adapter_gradient, adapter_down_factor.T, preferred_element_type=jnp.float32)
    query_grad = gate_gradient * conv_value
    conv_grad = gate_gradient * query
    count_blocks = MIXER_CHANNELS // channel_block
    stacked = conv_grad.T.reshape(count_blocks, channel_block, SEQUENCE_TOKENS)
    residue_blocks = mode_residue.reshape(count_blocks, channel_block, MODES)
    rate_blocks = mode_decay_rate.reshape(count_blocks, channel_block, MODES)
    long_corr = lax.map(correlate, (stacked, residue_blocks, rate_blocks)).reshape(MIXER_CHANNELS, SEQUENCE_TOKENS).T
    inner_grad = long_corr + direct_bias * conv_grad
    key_grad = inner_grad * value
    value_grad = inner_grad * key
    query_input_gradient = short_backward(query_grad, short_conv_filter[0]).astype(jnp.bfloat16)
    key_input_gradient = short_backward(key_grad, short_conv_filter[1]).astype(jnp.bfloat16)
    value_input_gradient = short_backward(value_grad, short_conv_filter[2]).astype(jnp.bfloat16)
    down_factor_gradient = adapter_scale * jnp.dot(gated_signal.T, adapter_gradient, preferred_element_type=jnp.float32) / math.sqrt(SEQUENCE_TOKENS)
    up_factor_gradient = adapter_scale * jnp.dot(adapter_activation.T, output_gradient, preferred_element_type=jnp.float32) / math.sqrt(SEQUENCE_TOKENS)
    return (query_input_gradient, key_input_gradient, value_input_gradient, down_factor_gradient, up_factor_gradient)
```

```python
import functools
import math

import jax
import jax.numpy as jnp
from jax import lax
from jax.experimental import pallas as pl
from jax.experimental.pallas import tpu as pltpu
from jax.sharding import PartitionSpec as P

adapter_scale = 2.0
MESH = pl.DeviceIdType.MESH
SEGMENTS = 8
LANES = 128
HALO = 16
MESSAGE = 24


def dot(left, right, left_axis, right_axis):
    return lax.dot_general(
        left,
        right,
        (((left_axis,), (right_axis,)), ((), ())),
        preferred_element_type=jnp.float32,
    )


def flipped(index, bit):
    return index + (1 - 2 * ((index // bit) % 2)) * bit


def kernel(
    n_ctx,
    n_tp,
    length,
    qp_any,
    kp_any,
    vp_any,
    lc_any,
    w_any,
    og_any,
    filt,
    bias,
    residue,
    rate,
    down,
    up,
    q_out,
    k_out,
    v_out,
    down_out,
    up_out,
    qp,
    kp,
    vp,
    lc,
    w,
    og,
    before,
    after,
    ext,
    query,
    key,
    value,
    gated,
    own,
    far_send,
    far_recv,
    x_send,
    x_recv,
    near_send,
    near_recv,
    rank_send,
    rank_recv,
    grad_send,
    grad_recv,
    g,
    qg,
    corr,
    g_lane,
    corr_lane,
    branch,
    decay,
    weight,
    seg,
    full,
    state,
    msg,
    msg_recv,
    load_sem,
    w_sem,
    halo_ss,
    halo_rs,
    far_ss,
    far_rs,
    x_ss,
    x_rs,
    near_ss,
    near_rs,
    rank_ss,
    rank_rs,
    grad_ss,
    grad_rs,
    msg_ss,
    msg_rs,
):
    tokens, channels = qp.shape
    half = channels // 2
    modes = rate.shape[0]
    rank = up.shape[0]
    step = tokens // SEGMENTS
    me = lax.axis_index("ctx")
    tp = lax.axis_index("tp")
    sibling = flipped(tp, 1)
    across = flipped(tp, 2)
    corner = flipped(sibling, 2)

    order = (corner, across, sibling, tp)

    def rows_of(block):
        return pl.ds(pl.multiple_of(block * channels, channels), channels)

    og_load = pltpu.make_async_copy(og_any, og, load_sem.at[0])
    og_load.start()
    w_loads = []
    for i, block in enumerate(order):
        load = pltpu.make_async_copy(w_any.at[rows_of(block)], w.at[i], w_sem.at[i])
        load.start()
        w_loads.append(load)
    loads = []
    for i, (src, dst) in enumerate(((qp_any, qp), (kp_any, kp), (vp_any, vp), (lc_any, lc))):
        load = pltpu.make_async_copy(src, dst, load_sem.at[i + 1])
        load.start()
        loads.append(load)

    barrier = pltpu.get_barrier_semaphore()
    for d in range(1, n_tp):
        pl.semaphore_signal(
            barrier, inc=1, device_id={"tp": lax.rem(tp + d, n_tp)}, device_id_type=MESH
        )
    for d in range(1, n_ctx):
        pl.semaphore_signal(
            barrier, inc=1, device_id={"ctx": lax.rem(me + d, n_ctx)}, device_id_type=MESH
        )

    rates = rate[...] / length
    decay[...] = jnp.exp(-rates)
    weight[...] = residue[...] * jnp.sqrt(rates)

    og_load.wait()
    og_value = og[...]
    low = dot(og_value, up[...], 1, 1)
    low16 = (adapter_scale * low).astype(jnp.bfloat16)
    rank_send[0, :rank] = dot(up[...], og_value, 1, 1)

    def product(i, h):
        columns = pl.ds(
            pl.multiple_of(order[i] * channels + h * half, half), half
        )
        return dot(og_value, w[i, h * half : (h + 1) * half], 1, 1) + dot(
            low16, down[:, columns], 1, 0
        )

    def remote(src, dst, ss, rs, where):
        return pltpu.make_async_remote_copy(
            src_ref=src,
            dst_ref=dst,
            send_sem=ss,
            recv_sem=rs,
            device_id=where,
            device_id_type=MESH,
        )

    w_loads[0].wait()
    far_send[0] = product(0, 0).astype(jnp.bfloat16)
    pl.semaphore_wait(barrier, n_tp + n_ctx - 2)

    far = [
        remote(far_send.at[h], far_recv.at[h], far_ss.at[h], far_rs.at[h], {"tp": sibling})
        for h in range(2)
    ]
    over = [
        remote(x_send.at[h], x_recv.at[h], x_ss.at[h], x_rs.at[h], {"tp": across})
        for h in range(2)
    ]
    near = [
        remote(near_send.at[h], near_recv.at[h], near_ss.at[h], near_rs.at[h], {"tp": sibling})
        for h in range(2)
    ]
    far[0].start()
    far_send[1] = product(0, 1).astype(jnp.bfloat16)
    far[1].start()
    w_loads[1].wait()
    for h in range(2):
        mine = product(1, h)
        far[h].wait_recv()
        x_send[h] = (mine + far_recv[h].astype(jnp.float32)).astype(jnp.bfloat16)
        over[h].start()

    for load in loads:
        load.wait()
    tails = [
        remote(
            src.at[pl.ds(tokens - HALO, HALO)],
            before.at[i],
            halo_ss.at[i],
            halo_rs.at[i],
            {"ctx": lax.rem(me + 1, n_ctx)},
        )
        for i, src in enumerate((qp, kp, vp))
    ]
    heads = [
        remote(
            src.at[pl.ds(0, HALO)],
            after.at[i],
            halo_ss.at[3 + i],
            halo_rs.at[3 + i],
            {"ctx": lax.rem(me + n_ctx - 1, n_ctx)},
        )
        for i, src in enumerate((kp, vp))
    ]

    @pl.when(me < n_ctx - 1)
    def _():
        for copy in tails:
            copy.start()

    @pl.when(me > 0)
    def _():
        for copy in heads:
            copy.start()

    w_loads[2].wait()
    for h in range(2):
        near_send[h] = product(2, h).astype(jnp.bfloat16)
        near[h].start()
    w_loads[3].wait()
    for h in range(2):
        own[:, h * half : (h + 1) * half] = product(3, h)

    @pl.when(me > 0)
    def _():
        for copy in tails:
            copy.wait_recv()

    @pl.when(me == 0)
    def _():
        before[...] = jnp.zeros_like(before)

    @pl.when(me < n_ctx - 1)
    def _():
        for copy in heads:
            copy.wait_recv()

    @pl.when(me == n_ctx - 1)
    def _():
        after[...] = jnp.zeros_like(after)

    def short_conv(index, src, dst, rows):
        ext[0:8] = before[index].astype(jnp.float32)[HALO - 8 :]
        ext[8 : 8 + tokens] = src[...].astype(jnp.float32)
        if index > 0:
            ext[8 + tokens : 16 + tokens] = after[index - 1].astype(jnp.float32)[:8]
        dst[0:rows] = (
            filt[index, 0:1] * ext[8 : 8 + rows]
            + filt[index, 1:2] * ext[7 : 7 + rows]
            + filt[index, 2:3] * ext[6 : 6 + rows]
        )

    short_conv(0, qp, query, tokens)
    gated[...] = (query[...] * lc[...].astype(jnp.float32)).astype(jnp.bfloat16)
    rank_send[0, rank:] = dot(down[:, rows_of(tp)], gated[...], 1, 1)

    rank_rounds = [
        remote(
            rank_send.at[k],
            rank_recv.at[k],
            rank_ss.at[k],
            rank_rs.at[k],
            {"tp": flipped(tp, 1 << k)},
        )
        for k in range(n_tp.bit_length() - 1)
    ]
    grad_rounds = [
        remote(
            grad_send.at[k],
            grad_recv.at[k],
            grad_ss.at[k],
            grad_rs.at[k],
            {"ctx": flipped(me, 1 << k)},
        )
        for k in range(n_ctx.bit_length() - 1)
    ]
    rank_rounds[0].start()
    short_conv(1, kp, key, tokens + 8)
    rank_rounds[0].wait_recv()
    rank_send[1] = rank_send[0] + rank_recv[0]
    rank_rounds[1].start()
    short_conv(2, vp, value, tokens + 8)

    msgs = []
    for h in range(2):
        near[h].wait_recv()
        over[h].wait_recv()
        lanes = slice(h * half, (h + 1) * half)
        gate = (
            own[:, lanes]
            + near_recv[h].astype(jnp.float32)
            + x_recv[h].astype(jnp.float32)
        )
        qg[0:tokens, lanes] = gate * lc[:, lanes].astype(jnp.float32)
        g[0:tokens, lanes] = gate * query[:, lanes]
        groups = range(h * half // LANES, (h + 1) * half // LANES)
        for group in groups:
            g_lane[group] = g[0:tokens, group * LANES : (group + 1) * LANES]
        for lane in range(h * half, (h + 1) * half, LANES):
            cols = pl.ds(lane, LANES)
            decays = [
                jnp.broadcast_to(decay[n : n + 1, cols], (SEGMENTS, LANES)) for n in range(modes)
            ]

            def back(i, held, group=lane // LANES, decays=decays):
                row = g_lane[group, pl.ds(step - 1 - i, SEGMENTS, stride=step), :]
                return tuple(a * x + row for a, x in zip(decays, held))

            zero = jnp.zeros((SEGMENTS, LANES), jnp.float32)
            held = lax.fori_loop(0, step - 1, back, (zero,) * modes, unroll=True)
            for n in range(modes):
                seg[lane // LANES, pl.ds(n, SEGMENTS, stride=modes), :] = held[n]
        a = decay[:, lanes]
        rest = jnp.exp(-rates[:, lanes] * (step - 1))
        ahead = jnp.zeros((modes, half), jnp.float32)
        for s in range(SEGMENTS - 1, -1, -1):
            local = [seg[group, s * modes : (s + 1) * modes] for group in groups]
            second = jnp.concatenate(local, axis=1) + rest * ahead
            ahead = a * second + g[s * step : s * step + 1, lanes]
            full[s * modes : (s + 1) * modes, lanes] = ahead
        msg[h, 0:modes] = second
        msg[h, modes : modes + 2] = g[0:2, lanes]
        msg[h, modes + 2 : modes + 4] = qg[0:2, lanes]
        msg[h, modes + 4 :] = jnp.zeros((MESSAGE - modes - 4, half), jnp.float32)
        for d in range(1, n_ctx):
            copy = remote(
                msg.at[h],
                msg_recv.at[d - 1, h],
                msg_ss.at[d - 1, h],
                msg_rs.at[d - 1, h],
                {"ctx": lax.rem(me + n_ctx - d, n_ctx)},
            )
            msgs.append((d, h, copy))

            @pl.when(me >= d)
            def _(copy=copy):
                copy.start()

    rank_rounds[1].wait_recv()
    sums = (rank_send[1] + rank_recv[1]).astype(jnp.bfloat16)
    grad_send[0, :rank] = dot(sums[:rank], gated[...], 1, 0)
    grad_send[0, rank:] = dot(sums[rank:], og_value, 1, 0)
    grad_rounds[0].start()

    def out_rows(index, src, dst, first, last):
        dst[first:last] = (
            filt[index, 0:1] * src[first:last]
            + filt[index, 1:2] * src[first + 1 : last + 1]
            + filt[index, 2:3] * src[first + 2 : last + 2]
        ).astype(jnp.bfloat16)

    out_rows(0, qg, q_out, 0, tokens - HALO)
    g[tokens:] = jnp.zeros((8, channels), jnp.float32)
    qg[tokens:] = jnp.zeros((8, channels), jnp.float32)
    corr[tokens:] = jnp.zeros((8, channels), jnp.float32)
    state[...] = jnp.zeros_like(state)
    for h in range(2):
        lanes = slice(h * half, (h + 1) * half)
        a = decay[:, lanes]
        for d, at, copy in msgs:
            if at != h:
                continue

            @pl.when(me + d < n_ctx)
            def _(d=d, copy=copy, lanes=lanes, a=a, h=h):
                copy.wait_recv()
                got = msg_recv[d - 1, h]
                if d == 1:
                    state[:, lanes] = got[:modes]
                    g[tokens : tokens + 2, lanes] = got[modes : modes + 2]
                    qg[tokens : tokens + 2, lanes] = got[modes + 2 : modes + 4]
                else:
                    gone = jnp.exp(-rates[:, lanes] * (tokens * (d - 1) - 1))
                    state[:, lanes] += gone * (a * got[:modes] + got[modes : modes + 1])

        second = state[:, lanes]
        first = a * second + g[tokens : tokens + 1, lanes]
        corr[tokens : tokens + 1, lanes] = jnp.sum(
            weight[:, lanes] * first, axis=0, keepdims=True
        )
        corr[tokens + 1 : tokens + 2, lanes] = jnp.sum(
            weight[:, lanes] * second, axis=0, keepdims=True
        )
        whole = jnp.exp(-rates[:, lanes] * step)
        carry = first
        for s in range(SEGMENTS - 1, -1, -1):
            at = slice(s * modes, (s + 1) * modes)
            for j in range(half // LANES):
                seg[h * half // LANES + j, at] = carry[:, j * LANES : (j + 1) * LANES]
            if s > 0:
                own_state = full[at, lanes]
                first = whole * first
                carry = own_state + first

        for lane in range(h * half, (h + 1) * half, LANES):
            cols = pl.ds(lane, LANES)
            decays = [
                jnp.broadcast_to(decay[n : n + 1, cols], (SEGMENTS, LANES)) for n in range(modes)
            ]
            weights = [
                jnp.broadcast_to(weight[n : n + 1, cols], (SEGMENTS, LANES)) for n in range(modes)
            ]

            def back(i, held, group=lane // LANES, decays=decays, weights=weights):
                at = pl.ds(step - 1 - i, SEGMENTS, stride=step)
                row = g_lane[group, at, :]
                held = tuple(a * x + row for a, x in zip(decays, held))
                terms = [b * x for b, x in zip(weights, held)]
                while len(terms) > 1:
                    terms = [
                        terms[j] + terms[j + 1] if j + 1 < len(terms) else terms[j]
                        for j in range(0, len(terms), 2)
                    ]
                corr_lane[group, at, :] = terms[0]
                return held

            start = tuple(
                seg[lane // LANES, pl.ds(n, SEGMENTS, stride=modes), :] for n in range(modes)
            )
            lax.fori_loop(0, step, back, start, unroll=True)
            corr[0:tokens, lane : lane + LANES] = corr_lane[lane // LANES]

    grad_now = grad_send[0]
    for k, copy in enumerate(grad_rounds):
        copy.wait_recv()
        grad_now = grad_now + grad_recv[k]
        if k + 1 < len(grad_rounds):
            grad_send[k + 1] = grad_now
            grad_rounds[k + 1].start()

    out_rows(0, qg, q_out, tokens - HALO, tokens)
    corr[...] = corr[...] + bias[...] * g[...]
    branch[...] = corr[...] * value[...]
    out_rows(1, branch, k_out, 0, tokens)
    branch[...] = corr[...] * key[...]
    out_rows(2, branch, v_out, 0, tokens)
    scale = adapter_scale / math.sqrt(length)
    down_out[...] = grad_now[:rank] * scale
    up_out[...] = grad_now[rank:] * scale

    for copy in far + over + near + rank_rounds + grad_rounds:
        copy.wait_send()

    @pl.when(me < n_ctx - 1)
    def _():
        for copy in tails:
            copy.wait_send()

    @pl.when(me > 0)
    def _():
        for copy in heads:
            copy.wait_send()

    for d, h, copy in msgs:

        @pl.when(me >= d)
        def _(copy=copy):
            copy.wait_send()


def on_device(
    n_ctx,
    n_tp,
    query_projected,
    key_projected,
    value_projected,
    long_conv_output,
    short_conv_filter,
    direct_bias,
    mode_residue,
    mode_decay_rate,
    output_weight,
    adapter_down_factor,
    adapter_up_factor,
    output_gradient,
):
    tokens, channels = query_projected.shape
    features = output_gradient.shape[1]
    modes = mode_residue.shape[1]
    rank = adapter_up_factor.shape[0]
    half = channels // 2
    f32, bf16 = jnp.float32, jnp.bfloat16
    rank_rounds = n_tp.bit_length() - 1
    grad_rounds = n_ctx.bit_length() - 1
    vmem = pl.BlockSpec(memory_space=pltpu.VMEM)
    anywhere = pl.BlockSpec(memory_space=pl.ANY)
    buffer = pltpu.VMEM
    dma = pltpu.SemaphoreType.DMA
    pair = (2, tokens, half)
    outs = pl.pallas_call(
        functools.partial(kernel, n_ctx, n_tp, tokens * n_ctx),
        out_shape=(
            jax.ShapeDtypeStruct((tokens, channels), bf16),
            jax.ShapeDtypeStruct((tokens, channels), bf16),
            jax.ShapeDtypeStruct((tokens, channels), bf16),
            jax.ShapeDtypeStruct((rank, channels), f32),
            jax.ShapeDtypeStruct((rank, features), f32),
        ),
        in_specs=[anywhere] * 6 + [vmem] * 6,
        out_specs=(vmem,) * 5,
        scratch_shapes=[
            buffer((tokens, channels), bf16),
            buffer((tokens, channels), bf16),
            buffer((tokens, channels), bf16),
            buffer((tokens, channels), bf16),
            buffer((n_tp, channels, features), bf16),
            buffer((tokens, features), bf16),
            buffer((3, HALO, channels), bf16),
            buffer((2, HALO, channels), bf16),
            buffer((tokens + 16, channels), f32),
            buffer((tokens, channels), f32),
            buffer((tokens + 8, channels), f32),
            buffer((tokens + 8, channels), f32),
            buffer((tokens, channels), bf16),
            buffer((tokens, channels), f32),
            buffer(pair, bf16),
            buffer(pair, bf16),
            buffer(pair, bf16),
            buffer(pair, bf16),
            buffer(pair, bf16),
            buffer(pair, bf16),
            buffer((rank_rounds, 2 * rank, tokens), f32),
            buffer((rank_rounds, 2 * rank, tokens), f32),
            buffer((grad_rounds, 2 * rank, channels), f32),
            buffer((grad_rounds, 2 * rank, channels), f32),
            buffer((tokens + 8, channels), f32),
            buffer((tokens + 8, channels), f32),
            buffer((tokens + 8, channels), f32),
            buffer((channels // LANES, tokens, LANES), f32),
            buffer((channels // LANES, tokens, LANES), f32),
            buffer((tokens + 8, channels), f32),
            buffer((modes, channels), f32),
            buffer((modes, channels), f32),
            buffer((channels // LANES, SEGMENTS * modes, LANES), f32),
            buffer((SEGMENTS * modes, channels), f32),
            buffer((modes, channels), f32),
            buffer((2, MESSAGE, half), f32),
            buffer((n_ctx - 1, 2, MESSAGE, half), f32),
            dma((5,)),
            dma((n_tp,)),
            dma((5,)),
            dma((5,)),
            dma((2,)),
            dma((2,)),
            dma((2,)),
            dma((2,)),
            dma((2,)),
            dma((2,)),
            dma((rank_rounds,)),
            dma((rank_rounds,)),
            dma((grad_rounds,)),
            dma((grad_rounds,)),
            dma((n_ctx - 1, 2)),
            dma((n_ctx - 1, 2)),
        ],
        compiler_params=pltpu.CompilerParams(
            collective_id=0, has_side_effects=True, vmem_limit_bytes=40 * 1024 * 1024
        ),
    )(
        query_projected,
        key_projected,
        value_projected,
        long_conv_output,
        output_weight,
        output_gradient,
        short_conv_filter,
        direct_bias.reshape(1, channels),
        mode_residue.T,
        mode_decay_rate.T,
        adapter_down_factor.T,
        adapter_up_factor,
    )
    return (outs[0], outs[1], outs[2], outs[3].T, outs[4])


def solution(mesh):
    in_specs = (
        P(("grp", "ctx"), "tp"),
        P(("grp", "ctx"), "tp"),
        P(("grp", "ctx"), "tp"),
        P(("grp", "ctx"), "tp"),
        P(None, None, "tp"),
        P("tp"),
        P("tp", None),
        P("tp", None),
        P(None, "tp"),
        P(),
        P(None, "tp"),
        P(("grp", "ctx"), "tp"),
    )
    out_specs = (
        P(("grp", "ctx"), "tp"),
        P(("grp", "ctx"), "tp"),
        P(("grp", "ctx"), "tp"),
        P(("grp", "tp"), None),
        P("grp", "tp"),
    )
    return jax.shard_map(
        functools.partial(on_device, mesh.shape["ctx"], mesh.shape["tp"]),
        mesh=mesh,
        in_specs=in_specs,
        out_specs=out_specs,
        check_vma=False,
    )
```

```python
import functools
import math

import jax
import jax.numpy as jnp
from jax import lax
from jax.experimental import pallas as pl
from jax.experimental.pallas import tpu as pltpu
from jax.sharding import PartitionSpec as P

adapter_scale = 2.0
MESH = pl.DeviceIdType.MESH
SEGMENTS = 8
LANES = 128
HALO = 16


def dot(left, right, left_axis, right_axis):
    return lax.dot_general(
        left,
        right,
        (((left_axis,), (right_axis,)), ((), ())),
        preferred_element_type=jnp.float32,
    )


def flipped(index, bit):
    return index + (1 - 2 * ((index // bit) % 2)) * bit


def kernel(
    n_ctx,
    n_tp,
    length,
    qp_any,
    kp_any,
    vp_any,
    lc_any,
    w_any,
    og_any,
    filt_any,
    bias_any,
    residue_any,
    rate_any,
    down_any,
    up_any,
    q_out,
    k_out,
    v_out,
    down_out,
    up_out,
    qp,
    kp,
    vp,
    lc,
    w,
    og,
    filt,
    bias,
    residue,
    rate,
    down,
    up,
    before,
    after,
    ext,
    query,
    key,
    value,
    gated,
    own,
    far_send,
    far_recv,
    x_send,
    x_recv,
    near_send,
    near_recv,
    rank_send,
    rank_recv,
    grad_send,
    grad_recv,
    g,
    qg,
    corr,
    g_lane,
    corr_lane,
    branch,
    decay,
    weight,
    seg,
    full,
    state,
    msg,
    msg_recv,
    far_msg,
    far_msg_recv,
    load_sem,
    w_sem,
    halo_ss,
    halo_rs,
    far_ss,
    far_rs,
    x_ss,
    x_rs,
    near_ss,
    near_rs,
    rank_ss,
    rank_rs,
    grad_ss,
    grad_rs,
    msg_ss,
    msg_rs,
):
    tokens, channels = qp.shape
    half = channels // 2
    modes = rate.shape[0]
    rank = up.shape[0]
    step = tokens // SEGMENTS
    me = lax.axis_index("ctx")
    tp = lax.axis_index("tp")
    sibling = flipped(tp, 1)
    across = flipped(tp, 2)
    corner = flipped(sibling, 2)

    barrier = pltpu.get_barrier_semaphore()
    for d in range(1, n_tp):
        pl.semaphore_signal(
            barrier, inc=1, device_id={"tp": lax.rem(tp + d, n_tp)}, device_id_type=MESH
        )
    for d in range(1, n_ctx):
        pl.semaphore_signal(
            barrier, inc=1, device_id={"ctx": lax.rem(me + d, n_ctx)}, device_id_type=MESH
        )

    order = (corner, across, sibling, tp)

    def rows_of(block):
        return pl.ds(pl.multiple_of(block * channels, channels), channels)

    first_loads = []
    for i, (src, dst) in enumerate(((og_any, og), (up_any, up), (down_any, down))):
        load = pltpu.make_async_copy(src, dst, load_sem.at[i])
        load.start()
        first_loads.append(load)
    w_loads = []
    for i, block in enumerate(order):
        load = pltpu.make_async_copy(w_any.at[rows_of(block)], w.at[i], w_sem.at[i])
        load.start()
        w_loads.append(load)
    loads = []
    for i, (src, dst) in enumerate(
        (
            (rate_any, rate),
            (residue_any, residue),
            (qp_any, qp),
            (kp_any, kp),
            (vp_any, vp),
            (lc_any, lc),
            (filt_any, filt),
            (bias_any, bias),
        )
    ):
        load = pltpu.make_async_copy(src, dst, load_sem.at[i + 3])
        load.start()
        loads.append(load)

    for load in first_loads:
        load.wait()
    og_value = og[...]
    low = dot(og_value, up[...], 1, 1)
    low16 = (adapter_scale * low).astype(jnp.bfloat16)
    rank_send[0, :rank] = dot(up[...], og_value, 1, 1)

    def product(i, h):
        columns = pl.ds(
            pl.multiple_of(order[i] * channels + h * half, half), half
        )
        return dot(og_value, w[i, h * half : (h + 1) * half], 1, 1) + dot(
            low16, down[:, columns], 1, 0
        )

    def remote(src, dst, ss, rs, where):
        return pltpu.make_async_remote_copy(
            src_ref=src,
            dst_ref=dst,
            send_sem=ss,
            recv_sem=rs,
            device_id=where,
            device_id_type=MESH,
        )

    far = [
        remote(far_send.at[h], far_recv.at[h], far_ss.at[h], far_rs.at[h], {"tp": sibling})
        for h in range(2)
    ]
    over = [
        remote(x_send.at[h], x_recv.at[h], x_ss.at[h], x_rs.at[h], {"tp": across})
        for h in range(2)
    ]
    near = [
        remote(near_send.at[h], near_recv.at[h], near_ss.at[h], near_rs.at[h], {"tp": sibling})
        for h in range(2)
    ]
    tails = [
        remote(
            src.at[pl.ds(tokens - HALO, HALO)],
            before.at[i],
            halo_ss.at[i],
            halo_rs.at[i],
            {"ctx": lax.rem(me + 1, n_ctx)},
        )
        for i, src in enumerate((qp, kp, vp))
    ]
    heads = [
        remote(
            src.at[pl.ds(0, HALO)],
            after.at[i],
            halo_ss.at[3 + i],
            halo_rs.at[3 + i],
            {"ctx": lax.rem(me + n_ctx - 1, n_ctx)},
        )
        for i, src in enumerate((kp, vp))
    ]

    for load in loads:
        load.wait()
    w_loads[0].wait()
    w_loads[1].wait()
    for h in range(2):
        far_send[h] = product(0, h).astype(jnp.bfloat16)
    pl.semaphore_wait(barrier, n_tp + n_ctx - 2)
    for h in range(2):
        far[h].start()

    @pl.when(me < n_ctx - 1)
    def _():
        for copy in tails:
            copy.start()

    @pl.when(me > 0)
    def _():
        for copy in heads:
            copy.start()

    for h in range(2):
        own[:, h * half : (h + 1) * half] = product(1, h)

    for i in range(2):
        w_loads[2 + i].wait()
    for h in range(2):
        near_send[h] = product(2, h).astype(jnp.bfloat16)
        near[h].start()
    for h in range(2):
        far[h].wait_recv()
        lanes = slice(h * half, (h + 1) * half)
        x_send[h] = (own[:, lanes] + far_recv[h].astype(jnp.float32)).astype(jnp.bfloat16)
        over[h].start()
    for h in range(2):
        own[:, h * half : (h + 1) * half] = product(3, h)
    rates = rate[...] / length
    decay[...] = jnp.exp(-rates)
    weight[...] = residue[...] * jnp.sqrt(rates)
    @pl.when(me > 0)
    def _():
        for copy in tails:
            copy.wait_recv()

    @pl.when(me == 0)
    def _():
        before[...] = jnp.zeros_like(before)

    @pl.when(me < n_ctx - 1)
    def _():
        for copy in heads:
            copy.wait_recv()

    @pl.when(me == n_ctx - 1)
    def _():
        after[...] = jnp.zeros_like(after)

    def short_conv(index, src, dst, rows):
        ext[0:8] = before[index].astype(jnp.float32)[HALO - 8 :]
        ext[8 : 8 + tokens] = src[...].astype(jnp.float32)
        if index > 0:
            ext[8 + tokens : 16 + tokens] = after[index - 1].astype(jnp.float32)[:8]
        dst[0:rows] = (
            filt[index, 0:1] * ext[8 : 8 + rows]
            + filt[index, 1:2] * ext[7 : 7 + rows]
            + filt[index, 2:3] * ext[6 : 6 + rows]
        )

    short_conv(0, qp, query, tokens)
    gated[...] = (query[...] * lc[...].astype(jnp.float32)).astype(jnp.bfloat16)
    rank_send[0, rank:] = dot(down[:, rows_of(tp)], gated[...], 1, 1)

    rank_rounds = [
        remote(
            rank_send.at[k],
            rank_recv.at[k],
            rank_ss.at[k],
            rank_rs.at[k],
            {"tp": flipped(tp, 1 << k)},
        )
        for k in range(n_tp.bit_length() - 1)
    ]
    grad_rounds = [
        remote(
            grad_send.at[k],
            grad_recv.at[k],
            grad_ss.at[k],
            grad_rs.at[k],
            {"ctx": flipped(me, 1 << k)},
        )
        for k in range(n_ctx.bit_length() - 1)
    ]
    rank_rounds[0].start()
    short_conv(1, kp, key, tokens + 8)
    short_conv(2, vp, value, tokens + 8)
    rank_rounds[0].wait_recv()
    rank_send[1] = rank_send[0] + rank_recv[0]
    rank_rounds[1].start()

    def adapter_gradients():
        rank_rounds[1].wait_recv()
        sums = (rank_send[1] + rank_recv[1]).astype(jnp.bfloat16)
        grad_send[0, :rank] = dot(sums[:rank], gated[...], 1, 0).astype(jnp.bfloat16)
        grad_send[0, rank:] = dot(sums[rank:], og_value, 1, 0).astype(jnp.bfloat16)
        grad_rounds[0].start()

    def next_grad_round(k):
        grad_rounds[k].wait_recv()
        total = grad_send[k].astype(jnp.float32) + grad_recv[k].astype(jnp.float32)
        if k + 1 < len(grad_rounds):
            grad_send[k + 1] = total.astype(jnp.bfloat16)
            grad_rounds[k + 1].start()
        return total

    msgs = []
    for h in range(2):
        near[h].wait_recv()
        over[h].wait_recv()
        lanes = slice(h * half, (h + 1) * half)
        gate = (
            own[:, lanes]
            + near_recv[h].astype(jnp.float32)
            + x_recv[h].astype(jnp.float32)
        )
        qg[0:tokens, lanes] = gate * lc[:, lanes].astype(jnp.float32)
        g[0:tokens, lanes] = gate * query[:, lanes]
        groups = range(h * half // LANES, (h + 1) * half // LANES)
        for group in groups:
            g_lane[group] = g[0:tokens, group * LANES : (group + 1) * LANES]
        for lane in range(h * half, (h + 1) * half, LANES):
            cols = pl.ds(lane, LANES)
            decays = [
                jnp.broadcast_to(decay[n : n + 1, cols], (SEGMENTS, LANES)) for n in range(modes)
            ]

            def back(i, held, group=lane // LANES, decays=decays):
                row = g_lane[group, pl.ds(step - 1 - i, SEGMENTS, stride=step), :]
                return tuple(a * x + row for a, x in zip(decays, held))

            zero = jnp.zeros((SEGMENTS, LANES), jnp.float32)
            held = lax.fori_loop(0, step - 1, back, (zero,) * modes, unroll=True)
            for n in range(modes):
                seg[lane // LANES, pl.ds(n, SEGMENTS, stride=modes), :] = held[n]
        a = decay[:, lanes]
        rest = jnp.exp(-rates[:, lanes] * (step - 1))
        ahead = jnp.zeros((modes, half), jnp.float32)
        for s in range(SEGMENTS - 1, -1, -1):
            local = [seg[group, s * modes : (s + 1) * modes] for group in groups]
            second = jnp.concatenate(local, axis=1) + rest * ahead
            ahead = a * second + g[s * step : s * step + 1, lanes]
            full[s * modes : (s + 1) * modes, lanes] = ahead
        msg[h, 0:modes] = second.astype(jnp.bfloat16)
        edges = jnp.concatenate(
            [g[0:2, lanes], qg[0:2, lanes], jnp.zeros((modes - 4, half), jnp.float32)], axis=0
        )
        msg[h, modes:] = edges.astype(jnp.bfloat16)
        far_msg[h] = ahead.astype(jnp.bfloat16)
        for d in range(1, n_ctx):
            copy = remote(
                msg.at[h] if d == 1 else far_msg.at[h],
                msg_recv.at[h] if d == 1 else far_msg_recv.at[d - 2, h],
                msg_ss.at[d - 1, h],
                msg_rs.at[d - 1, h],
                {"ctx": lax.rem(me + n_ctx - d, n_ctx)},
            )
            msgs.append((d, h, copy))

            @pl.when(me >= d)
            def _(copy=copy):
                copy.start()

        if h == 0:
            adapter_gradients()

    def out_rows(index, src, dst, first, last):
        dst[first:last] = (
            filt[index, 0:1] * src[first:last]
            + filt[index, 1:2] * src[first + 1 : last + 1]
            + filt[index, 2:3] * src[first + 2 : last + 2]
        ).astype(jnp.bfloat16)

    out_rows(0, qg, q_out, 0, tokens - HALO)
    for k in range(len(grad_rounds) - 1):
        next_grad_round(k)
    g[tokens:] = jnp.zeros((8, channels), jnp.float32)
    qg[tokens:] = jnp.zeros((8, channels), jnp.float32)
    corr[tokens:] = jnp.zeros((8, channels), jnp.float32)
    state[...] = jnp.zeros_like(state)
    for h in range(2):
        lanes = slice(h * half, (h + 1) * half)
        a = decay[:, lanes]
        for d, at, copy in msgs:
            if at != h:
                continue

            @pl.when(me + d < n_ctx)
            def _(d=d, copy=copy, lanes=lanes, h=h):
                copy.wait_recv()
                if d == 1:
                    got = msg_recv[h].astype(jnp.float32)
                    state[:, lanes] = got[:modes]
                    g[tokens : tokens + 2, lanes] = got[modes : modes + 2]
                    qg[tokens : tokens + 2, lanes] = got[modes + 2 : modes + 4]
                else:
                    gone = jnp.exp(-rates[:, lanes] * (tokens * (d - 1) - 1))
                    state[:, lanes] += gone * far_msg_recv[d - 2, h].astype(jnp.float32)

        second = state[:, lanes]
        first = a * second + g[tokens : tokens + 1, lanes]
        corr[tokens : tokens + 1, lanes] = jnp.sum(
            weight[:, lanes] * first, axis=0, keepdims=True
        )
        corr[tokens + 1 : tokens + 2, lanes] = jnp.sum(
            weight[:, lanes] * second, axis=0, keepdims=True
        )
        whole = jnp.exp(-rates[:, lanes] * step)
        carry = first
        for s in range(SEGMENTS - 1, -1, -1):
            at = slice(s * modes, (s + 1) * modes)
            for j in range(half // LANES):
                seg[h * half // LANES + j, at] = carry[:, j * LANES : (j + 1) * LANES]
            if s > 0:
                own_state = full[at, lanes]
                first = whole * first
                carry = own_state + first

        for lane in range(h * half, (h + 1) * half, LANES):
            cols = pl.ds(lane, LANES)
            decays = [
                jnp.broadcast_to(decay[n : n + 1, cols], (SEGMENTS, LANES)) for n in range(modes)
            ]
            weights = [
                jnp.broadcast_to(weight[n : n + 1, cols], (SEGMENTS, LANES)) for n in range(modes)
            ]

            def back(i, held, group=lane // LANES, decays=decays, weights=weights):
                at = pl.ds(step - 1 - i, SEGMENTS, stride=step)
                row = g_lane[group, at, :]
                held = tuple(a * x + row for a, x in zip(decays, held))
                terms = [b * x for b, x in zip(weights, held)]
                while len(terms) > 1:
                    terms = [
                        terms[j] + terms[j + 1] if j + 1 < len(terms) else terms[j]
                        for j in range(0, len(terms), 2)
                    ]
                corr_lane[group, at, :] = terms[0]
                return held

            start = tuple(
                seg[lane // LANES, pl.ds(n, SEGMENTS, stride=modes), :] for n in range(modes)
            )
            lax.fori_loop(0, step, back, start, unroll=True)
            corr[0:tokens, lane : lane + LANES] = corr_lane[lane // LANES]

    out_rows(0, qg, q_out, tokens - HALO, tokens)
    corr[...] = corr[...] + bias[...] * g[...]
    branch[...] = corr[...] * value[...]
    out_rows(1, branch, k_out, 0, tokens)
    branch[...] = corr[...] * key[...]
    out_rows(2, branch, v_out, 0, tokens)
    grad_now = next_grad_round(len(grad_rounds) - 1)
    scale = adapter_scale / math.sqrt(length)
    down_out[...] = grad_now[:rank] * scale
    up_out[...] = grad_now[rank:] * scale

    for copy in far + over + near + rank_rounds + grad_rounds:
        copy.wait_send()

    @pl.when(me < n_ctx - 1)
    def _():
        for copy in tails:
            copy.wait_send()

    @pl.when(me > 0)
    def _():
        for copy in heads:
            copy.wait_send()

    for d, h, copy in msgs:

        @pl.when(me >= d)
        def _(copy=copy):
            copy.wait_send()


def on_device(
    n_ctx,
    n_tp,
    query_projected,
    key_projected,
    value_projected,
    long_conv_output,
    short_conv_filter,
    direct_bias,
    mode_residue,
    mode_decay_rate,
    output_weight,
    adapter_down_factor,
    adapter_up_factor,
    output_gradient,
):
    tokens, channels = query_projected.shape
    features = output_gradient.shape[1]
    modes = mode_residue.shape[1]
    rank = adapter_up_factor.shape[0]
    half = channels // 2
    f32, bf16 = jnp.float32, jnp.bfloat16
    rank_rounds = n_tp.bit_length() - 1
    grad_rounds = n_ctx.bit_length() - 1
    vmem = pl.BlockSpec(memory_space=pltpu.VMEM)
    hbm = pl.BlockSpec(memory_space=pltpu.HBM)
    buffer = pltpu.VMEM
    dma = pltpu.SemaphoreType.DMA
    pair = (2, tokens, half)
    outs = pl.pallas_call(
        functools.partial(kernel, n_ctx, n_tp, tokens * n_ctx),
        out_shape=(
            buffer((tokens, channels), bf16),
            buffer((tokens, channels), bf16),
            buffer((tokens, channels), bf16),
            buffer((rank, channels), f32),
            buffer((rank, features), f32),
        ),
        in_specs=[hbm] * 12,
        out_specs=(vmem,) * 5,
        scratch_shapes=[
            buffer((tokens, channels), bf16),
            buffer((tokens, channels), bf16),
            buffer((tokens, channels), bf16),
            buffer((tokens, channels), bf16),
            buffer((n_tp, channels, features), bf16),
            buffer((tokens, features), bf16),
            buffer(short_conv_filter.shape, f32),
            buffer((1, channels), f32),
            buffer((modes, channels), f32),
            buffer((modes, channels), f32),
            buffer((rank, adapter_down_factor.shape[0]), bf16),
            buffer((rank, features), bf16),
            buffer((3, HALO, channels), bf16),
            buffer((2, HALO, channels), bf16),
            buffer((tokens + 16, channels), f32),
            buffer((tokens, channels), f32),
            buffer((tokens + 8, channels), f32),
            buffer((tokens + 8, channels), f32),
            buffer((tokens, channels), bf16),
            buffer((tokens, channels), f32),
            buffer(pair, bf16),
            buffer(pair, bf16),
            buffer(pair, bf16),
            buffer(pair, bf16),
            buffer(pair, bf16),
            buffer(pair, bf16),
            buffer((rank_rounds, 2 * rank, tokens), f32),
            buffer((rank_rounds, 2 * rank, tokens), f32),
            buffer((grad_rounds, 2 * rank, channels), bf16),
            buffer((grad_rounds, 2 * rank, channels), bf16),
            buffer((tokens + 8, channels), f32),
            buffer((tokens + 8, channels), f32),
            buffer((tokens + 8, channels), f32),
            buffer((channels // LANES, tokens, LANES), f32),
            buffer((channels // LANES, tokens, LANES), f32),
            buffer((tokens + 8, channels), f32),
            buffer((modes, channels), f32),
            buffer((modes, channels), f32),
            buffer((channels // LANES, SEGMENTS * modes, LANES), f32),
            buffer((SEGMENTS * modes, channels), f32),
            buffer((modes, channels), f32),
            buffer((2, 2 * modes, half), bf16),
            buffer((2, 2 * modes, half), bf16),
            buffer((2, modes, half), bf16),
            buffer((max(n_ctx - 2, 1), 2, modes, half), bf16),
            dma((11,)),
            dma((n_tp,)),
            dma((5,)),
            dma((5,)),
            dma((2,)),
            dma((2,)),
            dma((2,)),
            dma((2,)),
            dma((2,)),
            dma((2,)),
            dma((rank_rounds,)),
            dma((rank_rounds,)),
            dma((grad_rounds,)),
            dma((grad_rounds,)),
            dma((n_ctx - 1, 2)),
            dma((n_ctx - 1, 2)),
        ],
        compiler_params=pltpu.CompilerParams(
            collective_id=0, has_side_effects=True, vmem_limit_bytes=62 * 1024 * 1024
        ),
    )(
        query_projected,
        key_projected,
        value_projected,
        long_conv_output,
        output_weight,
        output_gradient,
        short_conv_filter,
        direct_bias.reshape(1, channels),
        mode_residue.T,
        mode_decay_rate.T,
        adapter_down_factor.T,
        adapter_up_factor,
    )
    return (outs[0], outs[1], outs[2], outs[3].T, outs[4])


def solution(mesh):
    in_specs = (
        P(("grp", "ctx"), "tp"),
        P(("grp", "ctx"), "tp"),
        P(("grp", "ctx"), "tp"),
        P(("grp", "ctx"), "tp"),
        P(None, None, "tp"),
        P("tp"),
        P("tp", None),
        P("tp", None),
        P(None, "tp"),
        P(),
        P(None, "tp"),
        P(("grp", "ctx"), "tp"),
    )
    out_specs = (
        P(("grp", "ctx"), "tp"),
        P(("grp", "ctx"), "tp"),
        P(("grp", "ctx"), "tp"),
        P(("grp", "tp"), None),
        P("grp", "tp"),
    )
    return jax.shard_map(
        functools.partial(on_device, mesh.shape["ctx"], mesh.shape["tp"]),
        mesh=mesh,
        in_specs=in_specs,
        out_specs=out_specs,
        check_vma=False,
    )
```
